32 devices in a mesh: seq: 8 (over z, x), crop: 4 (over y, core).
Axes of the slice: x: 2, y: 2, z: 4, core: 2. Of those that a mesh axis runs over, the one named last changes fastest.
Arguments:
- pair_state: bfloat16 [8, 256, 256, 128], P('crop', 'seq'), may hold values from -6 to 6
- crop_lengths: int32 [4, 2], P('crop'), may hold values from 64 to 256, as said below
- norm_gain: float32 [2, 3, 128], replicated, may hold values from 0.5 to 1.5
- norm_shift: float32 [2, 3, 128], replicated, may hold values from -1.5 to 1.5
- attend_weight: bfloat16 [2, 2, 128, 512], replicated, may hold values from -0.5 to 0.5
- gate_bias: float32 [2, 2, 128], replicated, may hold values from -4 to 4
- attend_output: bfloat16 [2, 2, 128, 128], replicated, may hold values from -4 to 4
- output_bias: float32 [2, 2, 128], replicated, may hold values from -1.5 to 1.5
- expand_weight: bfloat16 [2, 128, 512], replicated, may hold values from -0.5 to 0.5
- expand_bias: float32 [2, 512], replicated, may hold values from -2.5 to 2.5
- contract_weight: bfloat16 [2, 512, 128], replicated, may hold values from -0.5 to 0.5
- contract_bias: float32 [2, 128], replicated, may hold values from -1.5 to 1.5
- cotangent: bfloat16 [8, 256, 256, 128], P('crop', 'seq'), may hold values from -6 to 6
Outputs:
- pair_output: bfloat16 [8, 256, 256, 128], P('crop', 'seq')
- pair_grad: float32 [8, 256, 256, 128], P('crop', 'seq')
- grad_norm_gain: float32 [2, 3, 128], replicated
- grad_norm_shift: float32 [2, 3, 128], replicated
- grad_attend_weight: float32 [2, 2, 128, 512], replicated
- grad_gate_bias: float32 [2, 2, 128], replicated
- grad_attend_output: float32 [2, 2, 128, 128], replicated
- grad_output_bias: float32 [2, 2, 128], replicated
- grad_expand_weight: float32 [2, 128, 512], replicated
- grad_expand_bias: float32 [2, 512], replicated
- grad_contract_weight: float32 [2, 512, 128], replicated
- grad_contract_bias: float32 [2, 128], replicated
The draws below stay inside these ranges and needn't reach their ends.
Inputs may be any that keep to these rules, and one draw needn't show every extreme that they name: `crop_lengths`: each row holds the lengths of the 2 crops of one group; one of them, at a place that varies from group to group, equals 256, and the others lie between 64 and 256.
All inputs are finite; a program needn't handle non-finite values.
Results may differ from the reference program's by a relative error of at most 0.019.
Values may be sent and summed in bfloat16 or wider, within the bound.
No kernel may reach another device: no remote copies, remote signals or barrier semaphores. Data moves between devices by JAX's collectives and lax.ppermute only.
A program may use at most 768 MiB of HBM per device.

```python
import jax
import jax.numpy as jnp
from jax import lax

C = 128
HEADS = 4
HEAD_DIM = 32
FF = 512
L = 256
B = 2
LAYERS = 2
GROUPS = 4
CROPS = 8


def draw_crop_lengths(key, part):
    key = jax.random.fold_in(key, 11)
    length_key, place_key = jax.random.split(key)
    lengths = jax.random.randint(length_key, (GROUPS, B), L // 4, L + 1, dtype=jnp.int32)
    place = jax.random.randint(place_key, (GROUPS,), 0, B, dtype=jnp.int32)
    columns = jnp.arange(B, dtype=jnp.int32)
    lengths = jnp.where(columns[None, :] == place[:, None], L, lengths)
    return lengths.astype(jnp.int32)


def shard_levels(key, dims, cuts, smallest, top_value):
    gain, own = 1.0, jax.random.fold_in(key, 6)
    for position, blocks in cuts:
        steps = jnp.exp(jax.random.uniform(jax.random.fold_in(own, position), (blocks,), jnp.float32, smallest / len(cuts), top_value / len(cuts)))
        gain = gain * jnp.repeat(steps, dims[position] // blocks).reshape([-1 if axis == position else 1 for axis in range(len(dims))])
    return gain


def bell_draw(stream_key, dims, width, bound, shards=(), held_as=jnp.bfloat16):
    result = jax.random.normal(stream_key, dims, jnp.float32) * width
    if len(shards) > 0:
        result = shard_levels(stream_key, dims, shards, -0.22, 0.18) * result
    return jnp.clip(result, min=-bound, max=bound).astype(held_as)


def setup_inputs(seed: int = 0) -> dict:
    key_of = jax.random.split(jax.random.key(seed), 14)
    return {
        "pair_state": bell_draw(key_of[0], (CROPS, L, L, C), 1.0, 6.0, ((0, 4), (1, 8))),
        "crop_lengths": draw_crop_lengths(jax.random.fold_in(key_of[13], 71), 0),
        "norm_gain": jnp.clip(1.0 + 0.1 * jax.random.normal(key_of[2], (LAYERS, 3, C), jnp.float32), 0.5, 1.5),
        "norm_shift": bell_draw(key_of[3], (LAYERS, 3, C), 0.3, 1.5, (), jnp.float32),
        "attend_weight": bell_draw(key_of[4], (LAYERS, 2, C, 4 * C), C ** -0.5, 0.5),
        "gate_bias": bell_draw(key_of[5], (LAYERS, 2, C), 1.0, 4.0, (), jnp.float32),
        "attend_output": bell_draw(key_of[6], (LAYERS, 2, C, C), (max(C // 64, 1)) ** -0.5, 4.0),
        "output_bias": bell_draw(key_of[7], (LAYERS, 2, C), 0.3, 1.5, (), jnp.float32),
        "expand_weight": bell_draw(key_of[8], (LAYERS, C, FF), C ** -0.5, 0.5),
        "expand_bias": bell_draw(key_of[9], (LAYERS, FF), 0.5, 2.5, (), jnp.float32),
        "contract_weight": bell_draw(key_of[10], (LAYERS, FF, C), (FF // 4) ** -0.5, 0.5),
        "contract_bias": bell_draw(key_of[11], (LAYERS, C), 0.3, 1.5, (), jnp.float32),
        "cotangent": bell_draw(key_of[12], (CROPS, L, L, C), 1.0, 6.0, ((0, 4), (1, 8))),
    }


highest_precision = lax.Precision.HIGHEST
neg_big = -1000000000.0
gelu_coeff = 0.7978845608028654
row_block = 32

@jax.custom_vjp
def low(v):
    return lax.optimization_barrier(v.astype(jnp.bfloat16)).astype(jnp.float32)

@jax.custom_vjp
def low_back(v):
    return v

def low_keep(v):
    return (low(v), None)

def low_pass(kept, grad):
    return (grad,)

def back_keep(v):
    return (v, None)

def back_low(kept, grad):
    return (low(grad),)
low.defvjp(low_keep, low_pass)
low_back.defvjp(back_keep, back_low)

def layer_norm(x, scale_row, offset_row):
    average = lax.optimization_barrier(jnp.mean(x, axis=-1, keepdims=True))
    centred = x - average
    variance = lax.optimization_barrier(jnp.mean(centred * centred, axis=-1, keepdims=True))
    return centred * lax.rsqrt(variance + 1e-05) * scale_row + offset_row

def smooth_gate(t):
    return 0.5 * t * (1.0 + jnp.tanh(gelu_coeff * (t + 0.044715 * t * t * t)))

def attend(a, weight_in, gate_shift, weight_out, key_shift, rounded):

    def block(a_block):
        count = a_block.shape[0]
        h = low_back(jnp.einsum('xkc,cf->xkf', a_block, weight_in, precision=highest_precision))
        queries = low(h[..., :C]).reshape(count, L, HEADS, HEAD_DIM)
        keys_all = low(h[..., C:2 * C]).reshape(count, L, HEADS, HEAD_DIM)
        values = low(h[..., 2 * C:3 * C]).reshape(count, L, HEADS, HEAD_DIM)
        gates = jax.nn.sigmoid(h[..., 3 * C:] + gate_shift)
        scores = jnp.einsum('xqhd,xkhd->xhqk', queries, keys_all, precision=highest_precision) * HEAD_DIM ** (-0.5) + key_shift
        scores = low_back(scores)
        highest = lax.optimization_barrier(jnp.max(scores, axis=-1, keepdims=True))
        powers = jnp.exp(scores - highest)
        probability = powers / lax.optimization_barrier(jnp.sum(powers, axis=-1, keepdims=True))
        attended = jnp.einsum('xhqk,xkhd->xqhd', low(probability), values, precision=highest_precision).reshape(count, L, C)
        attended = low_back(attended)
        branch = jnp.einsum('xqc,cf->xqf', low(attended * gates), weight_out, precision=highest_precision)
        if rounded:
            return low_back(low(branch))
        return low_back(branch)
    blocks = a.reshape(L // row_block, row_block, L, C)
    return lax.map(jax.checkpoint(block), blocks).reshape(L, L, C)

def feed(a, expand_mat, expand_shift, contract_mat):

    def block(a_block):
        t = low_back(jnp.einsum('xkc,cf->xkf', a_block, expand_mat, precision=highest_precision) + expand_shift)
        r = low(smooth_gate(t))
        return low_back(jnp.einsum('xkf,fc->xkc', r, contract_mat, precision=highest_precision))
    blocks = a.reshape(L // row_block, row_block, L, C)
    return lax.map(jax.checkpoint(block), blocks).reshape(L, L, C)

def crop_forward(x, params, length):
    gains, offsets, attend_mats, gate_shift, output_mats, output_shift, expand_mat, expand_shift, contract_mat, contract_shift = params
    positions = jnp.arange(L)
    inside = (positions < length).astype(jnp.float32)
    key_shift = jnp.where(positions < length, 0.0, neg_big).astype(jnp.float32)
    pair_mask = (inside[:, None] * inside[None, :])[..., None]
    for layer_index in range(LAYERS):
        normed = layer_norm(x, gains[layer_index, 0], offsets[layer_index, 0])
        branch = attend(low(normed), attend_mats[layer_index, 0], gate_shift[layer_index, 0], output_mats[layer_index, 0], key_shift, False)
        x = x + (branch + output_shift[layer_index, 0]) * pair_mask
        normed = layer_norm(x, gains[layer_index, 1], offsets[layer_index, 1])
        turned = jnp.swapaxes(low_back(low(normed)), 0, 1)
        branch = jnp.swapaxes(attend(turned, attend_mats[layer_index, 1], gate_shift[layer_index, 1], output_mats[layer_index, 1], key_shift, True), 0, 1)
        x = x + (branch + output_shift[layer_index, 1]) * pair_mask
        normed = layer_norm(x, gains[layer_index, 2], offsets[layer_index, 2])
        branch = feed(low(normed), expand_mat[layer_index], expand_shift[layer_index], contract_mat[layer_index])
        x = x + (branch + contract_shift[layer_index]) * pair_mask
    return x

def reference(pair_state, crop_lengths, norm_gain, norm_shift, attend_weight, gate_bias, attend_output, output_bias, expand_weight, expand_bias, contract_weight, contract_bias, cotangent):
    params = tuple((w.astype(jnp.float32) for w in (norm_gain, norm_shift, attend_weight, gate_bias, attend_output, output_bias, expand_weight, expand_bias, contract_weight, contract_bias)))
    lengths = crop_lengths.reshape(-1).astype(jnp.int32)
    zeros = jax.tree.map(jnp.zeros_like, params)

    def one_crop(totals, pieces):
        state, length, cotan = pieces
        output, pullback = jax.vjp(lambda s, p: crop_forward(s, p, length), state.astype(jnp.float32), params)
        back_state, back_params = pullback(cotan.astype(jnp.float32))
        totals = jax.tree.map(lambda t, g: t + g, totals, back_params)
        return (totals, (output.astype(jnp.bfloat16), back_state))
    totals, (outputs, gradients) = lax.scan(one_crop, zeros, (pair_state, lengths, cotangent))
    return (outputs, gradients, totals[0], totals[1], totals[2], totals[3], totals[4], totals[5], totals[6], totals[7], totals[8], totals[9])
```

```python
import functools

import jax
import jax.numpy as jnp
from jax import lax
from jax.experimental import pallas as pl
from jax.experimental.pallas import tpu as pltpu
from jax.sharding import PartitionSpec as P

HEADS = 4
LOG2E = 1.4426950408889634
LN2 = 0.6931471805599453
GELU_A = 0.7978845608028654
GELU_B = 0.7978845608028654 * 0.044715
VMEM_BYTES = 63 * 1024 * 1024
CHUNK = 64
FORMS = {
    "cols_forward": (4, 1, 1),
    "away_forward": (8, 8, 0),
    "cols_middle": (8, 2, 4),
    "away_backward": (4, 4, 0),
    "cols_backward": (8, 2, 3),
    "rows_backward": (8, 1, 1),
}

f32 = jnp.float32
bf16 = jnp.bfloat16


def dot_nn(a, b):
    return lax.dot_general(a, b, (((1,), (0,)), ((), ())), preferred_element_type=f32)


def dot_nt(a, b):
    return lax.dot_general(a, b, (((1,), (1,)), ((), ())), preferred_element_type=f32)


def normalise(x):
    centred = x - jnp.mean(x, axis=0, keepdims=True)
    rstd = lax.rsqrt(jnp.mean(centred * centred, axis=0, keepdims=True) + 1e-5)
    return centred * rstd, rstd


def normalise_back(dy, unit, rstd, gain):
    scaled = dy * gain
    m1 = jnp.mean(scaled, axis=0, keepdims=True)
    m2 = jnp.mean(scaled * unit, axis=0, keepdims=True)
    return rstd * (scaled - m1 - unit * m2)


def row_live(L, length):
    return lax.broadcasted_iota(jnp.int32, (1, L), 1) < length


def rows_of(t, lead):
    t = t.T
    rows = t.shape[0] // functools.reduce(lambda x, y: x * y, lead)
    return t.reshape(lead + (rows, t.shape[1])).astype(bf16)


def pad_head(t, h, C):
    D = C // HEADS
    parts = []
    if h > 0:
        parts.append(jnp.zeros((h * D, t.shape[1]), bf16))
    parts.append(t[h * D : (h + 1) * D])
    if h < HEADS - 1:
        parts.append(jnp.zeros((C - (h + 1) * D, t.shape[1]), bf16))
    return jnp.concatenate(parts, axis=0)


def project(a, w_t, gate_b, length):
    C, L = a.shape
    h_t = dot_nn(w_t, a)
    yield
    live = row_live(L, length)
    keys = h_t[C : 2 * C]
    q_t = (h_t[:C] * (LOG2E * (C // HEADS) ** -0.5)).astype(bf16)
    k_t = jnp.where(live, keys, 0.0).astype(bf16)
    v_t = jnp.where(live, h_t[2 * C : 3 * C], 0.0)
    k = jnp.where(live, keys, keys[:, 0:1]).T.astype(bf16)
    g_t = 0.5 * jnp.tanh(0.5 * (h_t[3 * C :] + gate_b)) + 0.5
    return k, v_t.T.astype(bf16), q_t, k_t, v_t.astype(bf16), g_t


def chunk_of(opts):
    return 128 if "long" in opts else CHUNK


def in_chunks(rows, chunk, fn):
    if chunk is None:
        return fn(slice(0, rows))
    parts = [fn(slice(i, i + chunk)) for i in range(0, rows, chunk)]
    if isinstance(parts[0], tuple):
        return tuple(jnp.concatenate(p, axis=0) for p in zip(*parts))
    return jnp.concatenate(parts, axis=0)


def attend(k, q_t, v_t, length, chunk, lean):
    L, C = k.shape
    D = C // HEADS
    ones = jnp.where(row_live(L, length), 1.0, 0.0)
    ones = jnp.broadcast_to(ones, (16, L)).astype(bf16)
    scores = [dot_nn(k, pad_head(q_t, h, C)) for h in range(HEADS)]
    yield
    outs, powers, sums, mixes, tops = [], [], [], [], []
    for h in range(HEADS):
        s_t = scores[h]
        top = jnp.max(s_t, axis=0, keepdims=True)
        p = in_chunks(L, chunk, lambda r: jnp.exp2(s_t[r] - top).astype(bf16))
        powers.append(p)
        tops.append(top)
        mixes.append(dot_nn(jnp.concatenate([v_t[h * D : (h + 1) * D], ones], axis=0), p))
        if h % 2 == 1:
            yield
    for h in range(HEADS):
        o = mixes[h]
        inv = 1.0 / o[D : D + 1]
        outs.append(o[:D] * inv)
        sums.append(inv)
        if lean:
            tops[h] = tops[h] + jnp.log2(o[D : D + 1])
    return jnp.concatenate(outs, axis=0), powers, sums, tops


def attend_back(dz, a, kept, w, wo, length, chunk, dz_n, a_n):
    v, q_t, k_t, g_t, mixed_t, powers, sums = kept
    C, L = q_t.shape
    D = C // HEADS
    dmixed = dot_nn(wo, dz) if dz is not None else dot_nt(wo, dz_n)
    d_wo = dot_nt(mixed_t, dz) if dz_n is None else dot_nn(mixed_t, dz_n)
    lean = not isinstance(powers, list)
    if lean:
        scores = [dot_nn(powers, pad_head(q_t, h, C)) for h in range(HEADS)]
    yield
    g = g_t.astype(f32)
    both = dmixed * mixed_t.astype(f32)
    dgate = both * (1.0 - g)
    do = dmixed * g
    live_row = row_live(L, length)
    dps, centres, dos = [], [], []
    for h in range(HEADS):
        rows = slice(h * D, (h + 1) * D)
        scale = 1.0 if lean else sums[h]
        do_h = (do[rows] * scale).astype(bf16)
        centres.append(jnp.sum(both[rows], axis=0, keepdims=True) * scale)
        parts = []
        if h > 0:
            parts.append(jnp.zeros((h * D, L), bf16))
        parts.append(do_h)
        if h < HEADS - 1:
            parts.append(jnp.zeros((C - (h + 1) * D, L), bf16))
        dps.append(dot_nn(v, jnp.concatenate(parts, axis=0)))
        dos.append(do_h)
    yield
    dq, dk, dv = [], [], []
    for h in range(HEADS):
        rows = slice(h * D, (h + 1) * D)
        dp, centre = dps[h], centres[h]
        if lean:
            s_t, log = scores[h], sums[h]
            p = in_chunks(L, chunk, lambda r: jnp.exp2(s_t[r] - log).astype(bf16))
        else:
            p = powers[h][...]
        ds = in_chunks(L, chunk, lambda r: p[r] * (dp[r] - centre).astype(bf16))
        dv.append(dot_nt(dos[h], p))
        dk.append(dot_nt(q_t[rows], ds))
        dq.append(dot_nn(k_t[rows], ds))
        if h % 2 == 1:
            yield
    dq = jnp.concatenate(dq, axis=0) * (D**-0.5)
    dk = jnp.where(live_row, jnp.concatenate(dk, axis=0) * LN2, 0.0)
    dv = jnp.where(live_row, jnp.concatenate(dv, axis=0), 0.0)
    dh = jnp.concatenate([dq, dk, dv, dgate], axis=0).astype(bf16)
    da = dot_nn(w, dh)
    d_w = dot_nt(dh, a) if a_n is None else dot_nn(dh, a_n)
    yield
    return da, d_w, d_wo, dgate


def lane_fold(t):
    out = t[:, :128]
    for j in range(1, t.shape[1] // 128):
        out = out + t[:, j * 128 : (j + 1) * 128]
    return out


VECTORS = ("gain0", "shift0", "gain1", "shift1", "gain2", "shift2", "bo0", "bo1", "gate0", "gate1", "bc")


class Weights:
    def __init__(self, refs, m, feed, L):
        self.columns, self.next_columns = refs[0].at[0], refs[1].at[0]
        self.w, self.w_t, self.wo, self.wo_t = (r.at[0, 0] for r in refs[2:6])
        if feed:
            self.we, self.wc, self.we_t, self.wc_t = (r.at[0] for r in refs[6:10])
        self.m, self.L, self.made = m, L, {}

    def column(self, ref, key, i):
        if key not in self.made:
            t = ref[...][:, i : i + 1]
            self.made[key] = jnp.broadcast_to(t, (t.shape[0], self.L))
        return self.made[key]

    def vector(self, name):
        return self.column(self.columns, name, VECTORS.index(name))

    def norm(self, n):
        return self.vector(f"gain{n}"), self.vector(f"shift{n}")

    def norm_of_next(self):
        return self.column(self.next_columns, "next0", 0), self.column(self.next_columns, "next1", 1)

    def expand_bias(self, rows):
        C = self.columns.shape[0]
        block, start = divmod(rows.start, C)
        t = self.column(self.columns, block, len(VECTORS) + block)
        return t[start : start + rows.stop - rows.start]


def weight_inputs(arrays, l, m, feed):
    vectors = arrays[0]

    def layer(a):
        return (a, (1,) + a.shape[1:], lambda *_: (l,) + (0,) * (a.ndim - 1))

    def branch(a):
        return (a, (1, 1) + a.shape[2:], lambda *_: (l, m) + (0,) * (a.ndim - 2))

    out = [layer(vectors), (vectors, (1,) + vectors.shape[1:], lambda *_: (1, 0, 0))]
    out += [branch(a) for a in arrays[1:5]]
    if feed:
        out += [layer(a) for a in arrays[5:9]]
    return out


def unpack(block, scratch, width, offset):
    peers, count, S, C = block.shape

    def step(p, _):
        part = block[p].astype(f32).reshape(count * S, C)
        at = pl.multiple_of((p * width + offset) * S, 8)
        scratch[pl.ds(at, count * S), :] = part
        return 0

    lax.fori_loop(0, peers, step, 0)


def pick(scratch, s, L, S):
    return scratch[pl.ds(s, L, stride=S), :]


SAVED = ("v", "q_t", "k_t", "g_t", "mix_t", "p", "sums")
LEAN = ("v", "q_t", "k_t", "g_t", "mix_t", "k", "sums")


def load_saved(refs, at, lean=False):
    v, q_t, k_t, g_t, mixed_t = [r[at] for r in refs[:5]]
    sums = [refs[6][at + (slice(h, h + 1), slice(None))] for h in range(HEADS)]
    if lean:
        return v, q_t, k_t, g_t, mixed_t, refs[5][at], sums
    powers = [refs[5].at[at + (h,)] for h in range(HEADS)]
    return v, q_t, k_t, g_t, mixed_t, powers, sums


def attention_forward(a, wts, length, saved=None, at=None, lean=False):
    gate_b = wts.vector(f"gate{wts.m}")
    k, v, q_t, k_t, v_t, g_t = yield from project(a, wts.w_t[...], gate_b, length)
    g_b = g_t.astype(bf16)
    if saved is not None:
        for ref, value in zip(saved, (v, q_t, k_t, g_b)):
            ref[at] = value
    o_t, powers, sums, logs = yield from attend(k, q_t, v_t, length, CHUNK, lean)
    mixed_t = (o_t * g_t).astype(bf16)
    z = dot_nn(wts.wo_t[...], mixed_t)
    if saved is not None:
        saved[4][at] = mixed_t
        if lean:
            saved[5][at] = k
        for h in range(HEADS):
            if not lean:
                saved[5][at + (h,)] = powers[h]
            saved[6][at + (slice(h, h + 1), slice(None))] = logs[h] if lean else sums[h]
    yield
    return z, (v, q_t, k_t, g_b, mixed_t, powers, sums)


def attention_backward(dz, a, wts, length, kept, acc, dz_n=None, a_n=None, opts=()):
    da, d_w, d_wo, dgate = yield from attend_back(
        dz, a, kept, wts.w[...], wts.wo[...], length, chunk_of(opts), dz_n, a_n
    )
    acc.add("d_w", d_w)
    acc.add("d_wo", d_wo)
    acc.add("d_gate", lane_fold(dgate))
    return da


def turned(opts, dz, a, wts, length, kept, acc):
    if "turn" in opts:
        return attention_backward(dz, a, wts, length, kept, acc, dz.T, a.T, opts)
    return attention_backward(dz, a, wts, length, kept, acc, opts=opts)


def gelu_half(t, bias):
    u = (t + bias).astype(bf16)
    u2 = u * u
    return u * bf16(0.5), u2, jnp.tanh(u * (bf16(GELU_A) + bf16(GELU_B) * u2))


def activate(t, wts):
    def part(r):
        u_half, _, th = gelu_half(t[r], wts.expand_bias(r))
        return u_half * th + u_half

    return in_chunks(t.shape[0], CHUNK, part)


def activate_back(t, dr, wts):
    def part(r):
        u_half, u2, th = gelu_half(t[r], wts.expand_bias(r))
        r_part = u_half * th + u_half
        left = bf16(0.5) - bf16(0.5) * th
        slope = (bf16(1.0) - left) + r_part * left * (bf16(2.0 * GELU_A) + bf16(6.0 * GELU_B) * u2)
        return r_part, dr[r].astype(bf16) * slope

    return in_chunks(t.shape[0], CHUNK, part)


def with_ones(t):
    return jnp.concatenate([t, jnp.ones((16, t.shape[1]), t.dtype)], axis=0)


def feed_gradients(acc, dz, r, a2, dt, opts):
    d_wc = dot_nn(r, dz.T) if "turn" in opts else dot_nt(r, dz)
    d_we = dot_nt(with_ones(a2), dt)
    yield
    C = a2.shape[0]
    acc.add("d_wc", d_wc)
    acc.add("d_we", d_we[:C])
    acc.add("d_be", d_we[C : C + 8])


BLOCKS = ("d_w", "d_wo", "d_wc", "d_we")


def acc_layout(names, C, F):
    shapes = {"d_w": (4 * C, C), "d_wo": (C, C), "d_be": (8, F), "d_wc": (F, C), "d_we": (C, F)}
    layout, at = {}, 0
    for name in names:
        rows, cols = shapes.get(name, (C, 128))
        layout[name] = (at, rows, cols // 128)
        at += rows * (cols // 128)
    return layout, at


def packed_layout(names, C, F):
    layout, _ = acc_layout(names, C, F)
    out, at = {}, 0
    for name in names:
        if name in BLOCKS:
            out[name] = at
            at += layout[name][1] * layout[name][2]
    row = at
    for name in names:
        if name not in BLOCKS:
            out[name] = row
            row += F // 128 if name == "d_be" else 1
    return out, at + 16


def pack(sums, names, rows, C, F):
    def body(*refs):
        out, at = refs[-1], 0
        for ref, kernel in zip(refs, names):
            layout, _ = acc_layout(kernel, C, F)
            vectors = []
            for name in kernel:
                first, count, blocks = layout[name]
                if name in BLOCKS:
                    for i in range(0, count * blocks, 128):
                        out[at : at + 128, :] = ref[first + i : first + i + 128, :].astype(bf16)
                        at += 128
                elif name == "d_be":
                    vectors += [ref[first + j * 8 : first + j * 8 + 1, :] for j in range(blocks)]
                else:
                    t = ref[first : first + count, :]
                    vectors.append(jnp.sum(t.T, axis=0, keepdims=True))
            vectors += [jnp.zeros((16 - len(vectors), 128), f32)]
            out[at : at + 16, :] = jnp.concatenate(vectors, axis=0).astype(bf16)
            at += 16
        if at < rows:
            out[at:, :] = jnp.zeros((rows - at, 128), bf16)

    return pl.pallas_call(
        body,
        out_shape=jax.ShapeDtypeStruct((rows, 128), bf16),
        compiler_params=pltpu.CompilerParams(vmem_limit_bytes=VMEM_BYTES),
        name="pack",
    )(*sums)


class Acc:
    def __init__(self, ref, layout):
        self.ref, self.layout = ref, layout

    def add(self, name, value):
        at, rows, blocks = self.layout[name]
        for j in range(blocks):
            self.ref[at + j * rows : at + (j + 1) * rows, :] += value[:, j * 128 : (j + 1) * 128]


def run(kernel, name, grid, info, inputs, weights, outputs, scratch, flops, names=(), before=None, into=(), wait=()):
    arrays, l, m, feed = weights
    C, F = arrays[5].shape[-2:]
    into = dict(into)
    ins_w = weight_inputs(arrays, l, m, feed)
    L = arrays[9]
    layout, rows = acc_layout(names, C, F)
    const = lambda *_: (0, 0)
    ins_b = [(before, (rows, 128), const)] if before is not None else []
    all_ins = list(inputs) + ins_w + ins_b
    outs = list(outputs) + ([((rows, 128), f32, (rows, 128), const)] if names else [])
    n_in, n_w = len(inputs), len(ins_w)

    def body(info_ref, *refs):
        ins = refs[:n_in]
        wts = Weights(refs[n_in : n_in + n_w], m, feed, L)
        rest = refs[len(all_ins) + len(into) + len(wait) :]
        acc = None
        if names:
            total = rest[len(outputs)]
            acc = Acc(total, layout)
            first = pl.program_id(0) == 0
            for d in range(1, len(grid)):
                first = first & (pl.program_id(d) == 0)

            @pl.when(first)
            def _():
                if before is not None:
                    total[...] = refs[n_in + n_w][...]
                else:
                    total[...] = jnp.zeros_like(total)

        kernel(info_ref, ins, wts, rest[: len(outputs)], acc, rest[len(outs) :])

    moved = sum(a.size * a.dtype.itemsize for a, _, _ in all_ins)
    moved += sum(4 * s[0] * s[1] if len(s) == 2 else 2 * functools.reduce(lambda x, y: x * y, s) for s, _, _, _ in outs)
    res = pl.pallas_call(
        body,
        grid_spec=pltpu.PrefetchScalarGridSpec(
            num_scalar_prefetch=1,
            grid=grid,
            in_specs=[pl.BlockSpec(b, i) for _, b, i in all_ins]
            + [pl.BlockSpec(memory_space=pl.ANY)] * (len(into) + len(wait)),
            out_specs=[pl.BlockSpec(b, i) for _, _, b, i in outs],
            scratch_shapes=scratch,
        ),
        out_shape=[jax.ShapeDtypeStruct(s, d) for s, d, _, _ in outs],
        compiler_params=pltpu.CompilerParams(
            vmem_limit_bytes=VMEM_BYTES,
            dimension_semantics=("arbitrary",) * len(grid),
        ),
        cost_estimate=pl.CostEstimate(flops=int(flops), bytes_accessed=int(moved), transcendentals=0),
        input_output_aliases={1 + len(all_ins) + i: o for i, o in enumerate(into)},
        name=name,
    )(info, *[a for a, _, _ in all_ins], *[into[o] for o in into], *wait)
    return res


def clip(form, most):
    return (min(form[0], most),) + form[1:]


def saved_outputs(lead, lead_block, index, L, C, names=SAVED):
    out = []
    for name in names:
        tail, dt = ((L, C), bf16) if name in ("v", "k") else ((C, L), bf16)
        if name == "p":
            tail = (HEADS, L, L)
        if name == "sums":
            tail, dt = (HEADS, L), f32
        more = lambda *g, extra=len(tail) - 2: index(*g) + (0,) * extra
        out.append((lead + tail, dt, lead_block + tail, more))
    return out


def together(form, body):
    count, width, lag = form[:3]
    waiting = [(s // width * lag, body(s)) for s in range(count)]
    turn = 0
    while waiting:
        waiting = [(t, g) for t, g in waiting if t > turn or next(g, g) is not g]
        turn += 1


HOME = (
    "d_w", "d_wo", "d_gate", "d_bo", "d_gain", "d_shift", "d_gain2", "d_shift2",
    "d_bc", "d_be", "d_wc", "d_we",
)
NAMES_MIDDLE = HOME + ("d_bo0",)
NAMES_COLS = HOME + ("d_gain0", "d_shift0")
NAMES_AWAY = ("d_w", "d_wo", "d_gate")
NAMES_ROWS = NAMES_AWAY + ("d_bo", "d_gain", "d_shift")


def body(
    pair_state,
    crop_lengths,
    norm_gain,
    norm_shift,
    attend_weight,
    gate_bias,
    attend_output,
    output_bias,
    expand_weight,
    expand_bias,
    contract_weight,
    contract_bias,
    cotangent,
):
    B, R, L, C = pair_state.shape
    F = expand_weight.shape[-1]
    n, crops = lax.axis_size("seq"), lax.axis_size("crop")
    half = n // B
    M = 2 * half
    W = L // M
    parts = 2 if W % 32 == 0 else 1
    K = W // parts
    RP = 2 if R % 32 == 0 else 1
    S, SR = min(16, K), min(16, R // RP)
    both = ("seq", "crop")
    pairs = range(0, crops, 2)
    wide = [[s * crops + p + c for s in range(n) for c in range(2)] for p in pairs]
    near = [
        [s * crops + p + c for s in range(b * half, (b + 1) * half) for c in range(2)]
        for p in pairs
        for b in range(B)
    ]

    vectors = [norm_gain[:, 0], norm_shift[:, 0], norm_gain[:, 1], norm_shift[:, 1]]
    vectors += [norm_gain[:, 2], norm_shift[:, 2], output_bias[:, 0], output_bias[:, 1]]
    vectors += [gate_bias[:, 0], gate_bias[:, 1], contract_bias]
    vectors = jnp.concatenate([jnp.stack(vectors, axis=1), expand_bias.reshape(-1, F // C, C)], axis=1)
    arrays = (
        jnp.swapaxes(jnp.pad(vectors, ((0, 0), (0, 128 - vectors.shape[1]), (0, 0))), 1, 2),
        attend_weight,
        jnp.swapaxes(attend_weight, 2, 3),
        attend_output,
        jnp.swapaxes(attend_output, 2, 3),
        expand_weight,
        contract_weight,
        jnp.swapaxes(expand_weight, 1, 2),
        jnp.swapaxes(contract_weight, 1, 2),
        L,
    )
    me, group = lax.axis_index("seq"), lax.axis_index("crop")
    lens = crop_lengths[0].astype(jnp.int32)
    other = lax.ppermute(lens, "crop", [(c, c ^ 1) for c in range(crops)])
    info_rows = jnp.concatenate([lens, (me * R).astype(jnp.int32)[None]])
    first_col = ((me % half) * 2 + group % 2) * W
    info_cols = [
        jnp.stack([jnp.where(group % 2 == t, lens, other)[me // half], first_col.astype(jnp.int32)])
        for t in range(2)
    ]

    def swap(groups, x):
        return lax.all_to_all(
            x, both, split_axis=0, concat_axis=0, tiled=True, axis_index_groups=groups
        )

    def over_wide(x):
        return swap(wide, x.reshape((2 * n,) + x.shape[-3:]))

    def over_near(x):
        return swap(near, x)

    def after(x, y):
        cut = (0,) * x.ndim
        size = (1,) * (x.ndim - 2) + (min(8, x.shape[-2], y.shape[-2]), 128)
        from_y = lax.slice(y, (0,) * y.ndim, (1,) * (y.ndim - 2) + size[-2:])
        mine = lax.slice(x, cut, size) + 0.0 * from_y.reshape(size)
        return lax.dynamic_update_slice(x, mine.astype(x.dtype), cut)

    flops = 60 * 2 * 256**3

    def cot_part(x, c):
        return jnp.swapaxes(x.reshape(B, R, M, parts, K, C)[:, :, :, c], 1, 2)

    last = over_wide(cot_part(cotangent, 0))
    cot = [last]

    form = clip((8, 8, 0), SR)
    G = form[0]

    def rows_forward(info, ins, wts, outs, acc, scr):
        (x_ref,) = ins
        b, step = pl.program_id(0), pl.program_id(1)
        length = info[b]

        def one(s):
            row = info[B] + step * G + s
            x = x_ref[0, s].astype(f32).T
            gain, shift = wts.norm(0)
            unit, _ = normalise(x)
            a = (unit * gain + shift).astype(bf16)
            z, _ = yield from attention_forward(a, wts, length, outs[parts:], (0, s))
            live = row_live(L, jnp.where(row < length, length, 0))
            x1 = x + jnp.where(live, z + wts.vector("bo0"), 0.0)
            x1 = rows_of(x1, (M, parts))
            for c in range(parts):
                outs[c][0, :, s] = x1[:, c]

        together(form, one)

    lead = (B, R)
    at_row = lambda b, i, *_: (b, i, 0, 0)
    x1_spec = ((B, M, R, K, C), bf16, (1, M, G, K, C), lambda b, i, *_: (b, 0, i, 0, 0))
    res = run(
        rows_forward,
        "rows_forward",
        (B, R // G),
        info_rows,
        [(pair_state, (1, G, L, C), at_row)],
        (arrays, 0, 0, False),
        [x1_spec] * parts + saved_outputs(lead, (1, G), at_row, L, C),
        [],
        B * R * flops,
    )
    saved_r0 = res[parts:]
    x1 = [over_wide(after(t, last) if c == 0 else t) for c, t in enumerate(res[:parts])]

    scr_in = pltpu.VMEM((L * S + S, C), f32)

    class Step:
        def __init__(self, form, count, first):
            self.form = clip(form[:3], S)
            self.opts = form[3:]
            G = self.G = self.form[0]
            per = self.per = S // G
            self.first, self.count = first, count
            self.grid = (count // S, per)
            at_col = lambda i, j, *_: (i * per + j, 0, 0)
            at_send = lambda i, j, *_: (0, first // G + i * per + j, 0, 0)
            self.saved = saved_outputs((count,), (G,), at_col, L, C)
            self.lean = saved_outputs((count,), (G,), at_col, L, C, LEAN)
            self.bf16 = ((count, C, L), bf16, (G, C, L), at_col)
            self.rows = ((count, L, C), bf16, (G, L, C), at_col)
            self.send = ((M, W, W, C), bf16, (M, G, W, C), at_send)

        def send_wide(self, t, rows):
            per = self.per
            at = lambda i, j, *_: (0, t, i * per + j, 0, 0)
            return ((n, 2, K, rows, C), bf16, (n, 1, self.G, rows, C), at)

        def wide(self, x, t):
            x = x.reshape((n, 2) + x.shape[1:])
            return (x, (n, 1, R, S, C), lambda i, j, *_: (0, t, 0, i, 0))

        def near(self, x):
            first = self.first // S
            return (x, (M, W, S, C), lambda i, j, *_: (0, 0, first + i, 0))

        def live_at(self, info, s):
            length = info[0]
            step = pl.program_id(0) * self.per + pl.program_id(1)
            column = info[1] + self.first + step * self.G + s
            return length, row_live(L, jnp.where(column < length, length, 0))

        def picked(self, scratch, s):
            return pick(scratch, pl.program_id(1) * self.G + s, L, S)

    def at_first(fill):
        pl.when(pl.program_id(1) == 0)(fill)

    def with_blocks(arrays, specs):
        return [(a, s[2], s[3]) for a, s in zip(arrays, specs)]

    def cols_forward(st, info, ins, wts, outs, acc, scr):
        (x1_ref,) = ins
        a0_out, x1_out, x2_out, x3_out = outs[:4]
        at_first(lambda: unpack(x1_ref.at[:, 0], scr[0], R, 0))

        def one(s):
            length, live = st.live_at(info, s)
            x1 = st.picked(scr[0], s).T
            x1_out[s] = x1.astype(bf16)
            gain, shift = wts.norm(1)
            unit, _ = normalise(x1)
            a = (unit * gain + shift).astype(bf16)
            z, _ = yield from attention_forward(a, wts, length, outs[4:], (s,), True)
            x2 = x1 + jnp.where(live, z + wts.vector("bo1"), 0.0)
            x2_out[s] = x2.astype(bf16)
            gain, shift = wts.norm(2)
            unit, _ = normalise(x2)
            a2 = (unit * gain + shift).astype(bf16)
            t = dot_nn(wts.we_t[...], a2)
            yield
            y = dot_nn(wts.wc_t[...], activate(t, wts))
            yield
            x3 = x2 + jnp.where(live, y + wts.vector("bc"), 0.0)
            x3_out[s] = x3.astype(bf16)
            gain, shift = wts.norm_of_next()
            unit, _ = normalise(x3)
            a0_out[:, s] = rows_of(unit * gain + shift, (M,))

        together(st.form, one)

    a0_send, kept_c0, before_c = [None, None], {}, [cot[0]]
    for c in range(parts):
        for t in range(2):
            st = Step(FORMS["cols_forward"], K, c * K)
            a0_send[t], *kept_c0[t, c] = run(
                functools.partial(cols_forward, st),
                "cols_forward",
                st.grid,
                info_cols[t],
                [st.wide(x1[c], t)],
                (arrays, 0, 1, True),
                [st.send, st.bf16, st.bf16, st.bf16] + st.lean,
                [scr_in],
                K * flops * 2,
                into={0: a0_send[t]} if c else {},
                wait=before_c,
            )
            before_c = [kept_c0[t, c][0]]
    a0 = []
    for t in range(2):
        a0.append(over_near(a0_send[t]))

    def away_forward(st, info, ins, wts, outs, acc, scr):
        z_out, a0_out = outs[:2]
        at_first(lambda: unpack(ins[0], scr[0], W, 0))

        def one(s):
            a = st.picked(scr[0], s)
            a0_out[s] = a.astype(bf16)
            a = a.T.astype(bf16)
            z, _ = yield from attention_forward(a, wts, info[0], outs[2:], (s,))
            z_out[:, s] = rows_of(z, (M,))

        together(st.form, one)

    z0, kept_r1 = [], []
    for t in range(2):
        st = Step(FORMS["away_forward"], W, 0)
        z_send, *kept = run(
            functools.partial(away_forward, st),
            "away_forward",
            st.grid,
            info_cols[t],
            [st.near(a0[t])],
            (arrays, 1, 0, False),
            [st.send, st.rows] + st.saved,
            [scr_in],
            W * flops,
            wait=[k[0] for k in kept_r1],
        )
        z0.append(over_near(z_send))
        kept_r1.append(kept)

    def cols_middle(st, info, ins, wts, outs, acc, scr):
        z_ref, cot_ref, x_ref = ins
        dz_send, out_send, dx_out = outs

        def fill():
            unpack(z_ref, scr[0], W, 0)
            unpack(cot_ref.at[:, 0], scr[1], R, 0)

        at_first(fill)

        def one(s):
            length, live = st.live_at(info, s)
            z0 = st.picked(scr[0], s).T
            x1 = x_ref[s].astype(f32) + jnp.where(live, z0 + wts.vector("bo0"), 0.0)
            gain1, shift1 = wts.norm(1)
            unit1, rstd1 = normalise(x1)
            a1 = (unit1 * gain1 + shift1).astype(bf16)
            z, kept = yield from attention_forward(a1, wts, length)
            x2 = x1 + jnp.where(live, z + wts.vector("bo1"), 0.0)
            gain2, shift2 = wts.norm(2)
            unit2, rstd2 = normalise(x2)
            a2 = (unit2 * gain2 + shift2).astype(bf16)
            t = dot_nn(wts.we_t[...], a2)
            dx = st.picked(scr[1], s).T
            dy = jnp.where(live, dx, 0.0)
            dz = dy.astype(bf16)
            dr = dot_nn(wts.wc[...], dz)
            acc.add("d_bc", lane_fold(dy))
            yield
            r, dt = activate_back(t, dr, wts)
            y = dot_nn(wts.wc_t[...], r)
            da2 = dot_nn(wts.we[...], dt)
            yield from feed_gradients(acc, dz, r, a2, dt, st.opts)
            x3 = x2 + jnp.where(live, y + wts.vector("bc"), 0.0)
            out_send[:, 0, s] = rows_of(x3, (n,))
            acc.add("d_gain2", lane_fold(da2 * unit2))
            acc.add("d_shift2", lane_fold(da2))
            dx = dx + normalise_back(da2, unit2, rstd2, gain2)
            dy = jnp.where(live, dx, 0.0)
            acc.add("d_bo", lane_fold(dy))
            da1 = yield from turned(st.opts, dy.astype(bf16), a1, wts, length, kept, acc)
            acc.add("d_gain", lane_fold(da1 * unit1))
            acc.add("d_shift", lane_fold(da1))
            dx = dx + normalise_back(da1, unit1, rstd1, gain1)
            dx_out[s] = dx.astype(bf16)
            dy = jnp.where(live, dx, 0.0)
            acc.add("d_bo0", lane_fold(dy))
            dz_send[:, s] = rows_of(dy, (M,))

        together(st.form, one)

    if parts > 1:
        later, _ = lax.optimization_barrier((cotangent, x1[0]))
        cot.append(over_wide(cot_part(later, 1)))
    dz_send, out_sends, dx1, sum_m = [None, None], [], {}, None
    dz0, out_rows = [], []
    for c in range(parts):
        out_send = None
        for t in range(2):
            st = Step(FORMS["cols_middle"], K, c * K)
            into = {0: dz_send[t]} if c else {}
            if t:
                into[1] = out_send
            dz_send[t], out_send, dx1[t, c], sum_m = run(
                functools.partial(cols_middle, st),
                "cols_middle",
                st.grid,
                info_cols[t],
                [st.near(z0[t]), st.wide(cot[c], t), (kept_c0[t, c][2], (st.G, C, L), st.bf16[3])],
                (arrays, 1, 1, True),
                [st.send, st.send_wide(t, R), st.bf16],
                [scr_in, scr_in],
                K * flops * 4,
                NAMES_MIDDLE,
                sum_m,
                into,
                out_rows if t else [],
            )
        out_sends.append(out_send)
        if c == 0:
            out_rows.append(over_wide(out_send))
    for t in range(2):
        dz0.append(over_near(dz_send[t]))

    def away_backward(st, info, ins, wts, outs, acc, scr):
        (da_send,) = outs
        a_ref = ins[1]
        at_first(lambda: unpack(ins[0], scr[0], W, 0))

        def one(s):
            dz_n = st.picked(scr[0], s)
            dz = dz_n.T.astype(bf16) if "turn" in st.opts else None
            dz_n = dz_n.astype(bf16)
            kept = load_saved(ins[2:], (s,))
            da = yield from attention_backward(
                dz, None, wts, info[0], kept, acc, dz_n, a_ref[s], st.opts
            )
            da_send[:, s] = rows_of(da, (M,))

        together(st.form, one)

    da0, sum_r1 = [], None
    for t in range(2):
        st = Step(FORMS["away_backward"], W, 0)
        da_send, sum_r1 = run(
            functools.partial(away_backward, st),
            "away_backward",
            st.grid,
            info_cols[t],
            [st.near(dz0[t])] + with_blocks(kept_r1[t], [st.rows] + st.saved),
            (arrays, 1, 0, False),
            [st.send],
            [scr_in],
            W * flops * 2,
            NAMES_AWAY,
            sum_r1,
        )
        last = over_near(da_send)
        da0.append(last)

    def cols_backward(st, info, ins, wts, outs, acc, scr):
        da_ref, dx_ref, x1_ref, x2_ref, x3_ref = ins[:5]
        at_first(lambda: unpack(da_ref, scr[0], W, 0))

        def one(s):
            length, live = st.live_at(info, s)
            da0 = st.picked(scr[0], s).T
            gain, _ = wts.norm_of_next()
            unit, rstd = normalise(x3_ref[s].astype(f32))
            acc.add("d_gain0", lane_fold(da0 * unit))
            acc.add("d_shift0", lane_fold(da0))
            dx = dx_ref[s].astype(f32) + normalise_back(da0, unit, rstd, gain)
            dy = jnp.where(live, dx, 0.0)
            gain2, shift2 = wts.norm(2)
            unit2, rstd2 = normalise(x2_ref[s].astype(f32))
            a2 = (unit2 * gain2 + shift2).astype(bf16)
            t = dot_nn(wts.we_t[...], a2)
            dz = dy.astype(bf16)
            dr = dot_nn(wts.wc[...], dz)
            acc.add("d_bc", lane_fold(dy))
            yield
            r, dt = activate_back(t, dr, wts)
            da2 = dot_nn(wts.we[...], dt)
            yield from feed_gradients(acc, dz, r, a2, dt, st.opts)
            acc.add("d_gain2", lane_fold(da2 * unit2))
            acc.add("d_shift2", lane_fold(da2))
            dx = dx + normalise_back(da2, unit2, rstd2, gain2)
            dy = jnp.where(live, dx, 0.0)
            acc.add("d_bo", lane_fold(dy))
            gain1, shift1 = wts.norm(1)
            unit1, rstd1 = normalise(x1_ref[s].astype(f32))
            a1 = (unit1 * gain1 + shift1).astype(bf16)
            kept = load_saved(ins[5:], (s,), True)
            da1 = yield from turned(st.opts, dy.astype(bf16), a1, wts, length, kept, acc)
            acc.add("d_gain", lane_fold(da1 * unit1))
            acc.add("d_shift", lane_fold(da1))
            dx = dx + normalise_back(da1, unit1, rstd1, gain1)
            dx = rows_of(dx, (n, len(outs)))
            for part, dx_send in enumerate(outs):
                dx_send[:, 0, s] = dx[:, part]

        together(st.form, one)

    if parts > 1:
        last = over_wide(after(out_sends[1], last))
        out_rows.append(last)
    dx_rows, sum_c0 = [], None
    for c in range(parts):
        pieces = RP if c == parts - 1 else 1
        dx_sends = []
        for t in range(2):
            st = Step(FORMS["cols_backward"], K, c * K)
            *dx_sends, sum_c0 = run(
                functools.partial(cols_backward, st),
                "cols_backward",
                st.grid,
                info_cols[t],
                [st.near(da0[t]), (dx1[t, c], (st.G, C, L), st.bf16[3])]
                + with_blocks(kept_c0[t, c], [st.bf16, st.bf16, st.bf16] + st.lean),
                (arrays, 0, 1, True),
                [st.send_wide(t, R // pieces)] * pieces,
                [scr_in],
                K * flops * 3,
                NAMES_COLS,
                sum_c0,
                dict(enumerate(dx_sends)),
            )
        sent = []
        for x in dx_sends:
            last = over_wide(after(x, last))
            sent.append(last.reshape((B, M) + last.shape[1:]))
        dx_rows.append(sent)

    def rows_backward(part, form, info, ins, wts, outs, acc, scr):
        x_ref = ins[parts]
        grad_out = outs[0]
        G = form[0]
        per = SR // G
        i, j = pl.program_id(1), pl.program_id(2)
        length = info[pl.program_id(0)]

        def fill():
            for c in range(parts):
                unpack(ins[c].at[0], scr[0], W, c * K)

        pl.when(j == 0)(fill)

        def one(s):
            row = info[B] + part * (R // RP) + (i * per + j) * G + s
            live = row_live(L, jnp.where(row < length, length, 0))
            dx = pick(scr[0], j * G + s, L, SR).T
            dy = jnp.where(live, dx, 0.0)
            acc.add("d_bo", lane_fold(dy))
            gain, shift = wts.norm(0)
            unit, rstd = normalise(x_ref[0, s].astype(f32).T)
            a = (unit * gain + shift).astype(bf16)
            kept = load_saved(ins[parts + 1 : parts + 1 + len(SAVED)], (0, s))
            da = yield from turned(form[3:], dy.astype(bf16), a, wts, length, kept, acc)
            acc.add("d_gain", lane_fold(da * unit))
            acc.add("d_shift", lane_fold(da))
            grad_out[0, s] = (dx + normalise_back(da, unit, rstd, gain)).T

        together(form, one)

    packed = [sum_m, sum_r1, sum_c0]
    pair_grad, sum_r0 = None, None
    for part in range(RP):
        form = clip(FORMS["rows_backward"], SR)
        G = form[0]
        per, steps = SR // G, R // RP // G
        at_row3 = lambda b, i, j, *_, o=part * steps: (b, o + i * per + j, 0, 0)
        sent = []
        for pieces in dx_rows:
            offset = part * (R // RP // SR) if len(pieces) == 1 else 0
            piece = pieces[0] if len(pieces) == 1 else pieces[part]
            sent.append(
                (piece, (1, M, K, SR, C), lambda b, i, j, *_, o=offset: (b, 0, 0, o + i, 0))
            )
        pair_grad, sum_r0 = run(
            functools.partial(rows_backward, part, form),
            "rows_backward",
            (B, R // RP // SR, per),
            info_rows,
            sent
            + [(pair_state, (1, G, L, C), at_row3)]
            + with_blocks(saved_r0, saved_outputs(lead, (1, G), at_row3, L, C)),
            (arrays, 0, 0, False),
            [((B, R, L, C), f32, (1, G, L, C), at_row3)],
            [pltpu.VMEM((L * SR + SR, C), f32)],
            B * (R // RP) * flops * 2,
            NAMES_ROWS,
            sum_r0,
            {0: pair_grad} if part else {},
        )
    out = jnp.stack([x.reshape(B, M, K, R, C) for x in out_rows], axis=2)
    pair_output = jnp.transpose(out.reshape(B, L, R, C), (0, 2, 1, 3))

    devices = n * crops

    def for_all(sums, names):
        rows = sum(packed_layout(x, C, F)[1] for x in names)
        rows = -(-rows // (devices * 16)) * 16
        return pack(sums, names, devices * rows, C, F).reshape(devices, rows, 128)

    def exchange(x):
        got = lax.all_to_all(x, both, 0, 0, tiled=True)
        return jnp.sum(got.astype(f32), axis=0)

    def spread(x, groups):
        x = jnp.broadcast_to(x, (len(groups[0]),) + x.shape)
        return swap(groups, x)

    first = for_all(packed, (NAMES_MIDDLE, NAMES_AWAY, NAMES_COLS))
    large = exchange(after(first, last))
    small = exchange(after(for_all([sum_r0], (NAMES_ROWS,)), large[None]))
    mine = jnp.concatenate([large, small], axis=0).astype(bf16)
    lines = [[s * crops + q for s in range(x, n, 2)] for x in range(2) for q in range(crops)]
    planes = [[s * crops + q for s in (z, z + 1) for q in range(crops)] for z in range(0, n, 2)]
    whole = spread(spread(mine, lines), planes)
    whole = whole.reshape(2 * crops, n // 2, mine.shape[0], 128)
    grads = assemble(whole, large.shape[0], C, F)
    gain, shift = (jnp.swapaxes(t, 0, 1) for t in grads[:2])
    return (pair_output, pair_grad, gain, shift) + tuple(grads[2:])


def assemble(whole, split, C, F):
    per_plane, planes, rows, _ = whole.shape
    tail_rows = rows - split
    names = (NAMES_MIDDLE, NAMES_AWAY, NAMES_COLS, NAMES_ROWS)
    layouts = [packed_layout(x, C, F) for x in names]
    bases = [0, layouts[0][1], layouts[0][1] + layouts[1][1]]

    def body(x_ref, gain, shift, w, gate, wo, bo, we, be, wc, bc, big, tail):
        def step(i, _):
            for z in range(planes):
                part = x_ref[i, z].astype(f32)
                at = z * per_plane + i
                big[pl.ds(pl.multiple_of(at * split, 16), split), :] = part[:split]
                tail[pl.ds(pl.multiple_of(at * tail_rows, 16), tail_rows), :] = part[split:]
            return 0

        lax.fori_loop(0, per_plane, step, 0)

        def get(kernel, name, count=1, offset=0):
            at = layouts[kernel][0][name] + offset
            if kernel == 3:
                return tail[at : at + count, :]
            return big[bases[kernel] + at : bases[kernel] + at + count, :]

        M, A, N, R = range(4)
        for l, m, kernel in ((0, 0, R), (0, 1, N), (1, 0, A), (1, 1, M)):
            for j in range(4):
                w[l, m, :, j * C : (j + 1) * C] = get(kernel, "d_w", C, j * C).T
            wo[l, m] = get(kernel, "d_wo", C)
            gate[l, m : m + 1, :] = get(kernel, "d_gate")
        for l, m, kernel, name in ((0, 0, R, "d_bo"), (0, 1, N, "d_bo"), (1, 0, M, "d_bo0"), (1, 1, M, "d_bo")):
            bo[l, m : m + 1, :] = get(kernel, name)
        where = ((0, 0, R, ""), (0, 1, N, ""), (0, 2, N, "2"), (1, 0, N, "0"), (1, 1, M, ""), (1, 2, M, "2"))
        for l, i, kernel, end in where:
            gain[i, l : l + 1, :] = get(kernel, "d_gain" + end)
            shift[i, l : l + 1, :] = get(kernel, "d_shift" + end)
        for l, kernel in ((0, N), (1, M)):
            bc[l : l + 1, :] = get(kernel, "d_bc")
            wc[l] = get(kernel, "d_wc", F)
            for j in range(F // 128):
                lanes = slice(j * 128, (j + 1) * 128)
                we[l, :, lanes] = get(kernel, "d_we", C, j * C)
                be[l : l + 1, lanes] = get(kernel, "d_be", 1, j)

    shapes = [(3, 2, C), (3, 2, C), (2, 2, C, 4 * C), (2, 2, C), (2, 2, C, C), (2, 2, C)]
    shapes += [(2, C, F), (2, F), (2, F, C), (2, C)]
    return pl.pallas_call(
        body,
        out_shape=[jax.ShapeDtypeStruct(s, f32) for s in shapes],
        scratch_shapes=[
            pltpu.VMEM((per_plane * planes * split, 128), f32),
            pltpu.VMEM((per_plane * planes * tail_rows, 128), f32),
        ],
        compiler_params=pltpu.CompilerParams(vmem_limit_bytes=VMEM_BYTES),
        name="assemble",
    )(whole)


def solution(mesh):
    placed = P("crop", "seq", None, None)
    return jax.shard_map(
        body,
        mesh=mesh,
        in_specs=(placed, P("crop", None)) + (P(),) * 10 + (placed,),
        out_specs=(placed, placed) + (P(),) * 10,
        check_vma=False,
    )
```
